256 devices in a mesh: dp: 8 (over y, x_hi), tensor: 32 (over z, x_lo, core).
Axes of the slice: x: 4 (x_hi: 2, x_lo: 2; x = x_hi * 2 + x_lo), y: 4, z: 8, core: 2. Of those that a mesh axis runs over, the one named last changes fastest.
Arguments:
- tokens: bfloat16 [2048, 5120], P('dp', 'tensor'), may hold values from -6 to 6
- out_grad: bfloat16 [2048, 5120], P('dp', 'tensor'), may hold values from -6 to 6
- master: float32 [3, 12800, 5120], P(None, 'tensor', 'dp'), may hold values from -50 to 50
- moment_first: float32 [3, 12800, 5120], P(None, 'tensor', 'dp'), may hold values from -10 to 10
- moment_second: float32 [3, 12800, 5120], P(None, 'tensor', 'dp'), may hold values from 0.01 to 0.1
Outputs:
- token_grad: bfloat16 [2048, 5120], P('dp', 'tensor')
- scaled_step: float32 [3, 12800, 5120], P(None, 'tensor', 'dp')
The draws below stay inside these ranges and needn't reach their ends.
All inputs are finite; a program needn't handle non-finite values.
Results may differ from the reference program's by a relative error of at most 0.029.
Values may be sent and summed in bfloat16 or wider, within the bound.
No kernel may reach another device: no remote copies, remote signals or barrier semaphores. Data moves between devices by JAX's collectives and lax.ppermute only.
A program may use at most 128 MiB of HBM per device.

```python
import math
import jax
import jax.numpy as jnp
from jax import lax

D = 5120
FF = 12800
TOK_GROUP = 256
TOKENS = 2048
N_DP = 8
N_TENSOR = 32


def spread_scale(key, col_slope):
    row_key, col_key = jax.random.split(key)
    row_part = jax.random.uniform(row_key, (3, FF, 1), jnp.float32, -0.6, 0.6)
    col_part = jax.random.uniform(col_key, (3, 1, D), jnp.float32, -0.6, 0.6)
    row_place = (jnp.arange(FF, dtype=jnp.float32) + 0.5) / FF - 0.5
    col_place = (jnp.arange(D, dtype=jnp.float32) + 0.5) / D - 0.5
    rising = math.log(3.0) * row_place[None, :, None] + col_slope * col_place[None, None, :]
    return jnp.exp(rising + row_part + col_part)


def draw_master(key, part):
    key = jax.random.fold_in(key, 11)
    base_key, scale_key = jax.random.split(key, 2)
    scale = spread_scale(scale_key, math.log(3.0))
    base = jnp.clip(jax.random.normal(base_key, (3, FF, D), jnp.float32), -5.0, 5.0)
    return (base * scale).astype(jnp.float32)


def draw_moment_first(key, part):
    key = jax.random.fold_in(key, 12)
    base_key, scale_key = jax.random.split(key)
    scale = 0.1 * spread_scale(scale_key, -math.log(6.0))
    base = jnp.clip(jax.random.normal(base_key, (3, FF, D), jnp.float32), -5.0, 5.0)
    return (base * scale).astype(jnp.float32)


def block_levels(stream_key, extent, shards, low, largest):
    def one(dim, shards_of):
        draws = jax.random.uniform(jax.random.fold_in(jax.random.fold_in(stream_key, 6), dim), (shards_of,), jnp.float32, low / len(shards), largest / len(shards))
        return jnp.repeat(jnp.exp(draws), extent[dim] // shards_of).reshape((-1,) + (1,) * (len(extent) - dim - 1))

    factor_of = one(*shards[0])
    for cut in shards[1:]:
        factor_of = factor_of * one(*cut)
    return factor_of


def bell_draw(key, dims, scale, most, shards=(), held_as=jnp.bfloat16):
    values = jax.random.normal(key, dims, jnp.float32) * scale
    if len(shards) > 0:
        values = block_levels(key, dims, shards, -0.22, 0.18) * values
    return jnp.clip(values, min=-most, max=most).astype(held_as)


def setup_inputs(seed: int = 0) -> dict:
    key_list = jax.random.split(jax.random.key(seed), 6)
    tokens = bell_draw(key_list[0], (TOKENS, D), 1.0, 6.0, ((0, 8), (1, 32)))
    out_grad = bell_draw(key_list[1], (TOKENS, D), 1.0, 6.0, ((0, 8), (1, 32)))
    master = draw_master(jax.random.fold_in(key_list[5], 71), 0)
    moment_first = draw_moment_first(jax.random.fold_in(key_list[5], 71), 0)
    moment_second = jnp.clip(jnp.exp(math.log(0.1) - 2.3025851 * jax.random.uniform(key_list[4], (3, FF, D), jnp.float32) ** block_levels(key_list[4], (3, FF, D), ((1, 32), (2, 8)), -0.2, 0.2)), 0.01, 0.1)
    return dict(tokens=tokens, out_grad=out_grad, master=master, moment_first=moment_first, moment_second=moment_second)


beta_first = 0.9
beta_second = 0.95
epsilon = 1e-06
weight_decay = 0.1
step_power = 3.0

def contract_rows(left, right):
    return lax.dot_general(left, right, (((0,), (0,)), ((), ())), preferred_element_type=jnp.float32)

def reference(tokens, out_grad, master, moment_first, moment_second):
    scale_in = D ** (-0.5)
    scale_out = FF ** (-0.5)
    weights = master.astype(jnp.bfloat16)
    gate_pre = scale_in * jnp.dot(tokens, weights[0].T, preferred_element_type=jnp.float32)
    up_pre = scale_in * jnp.dot(tokens, weights[1].T, preferred_element_type=jnp.float32)
    hid_grad = scale_out * jnp.dot(out_grad, weights[2].T, preferred_element_type=jnp.float32)
    sigmoid_gate = jax.nn.sigmoid(gate_pre)
    swish_gate = gate_pre * sigmoid_gate
    hidden = (swish_gate * up_pre).astype(jnp.bfloat16)
    gate_grad = (hid_grad * up_pre * sigmoid_gate * (1.0 + gate_pre * (1.0 - sigmoid_gate))).astype(jnp.bfloat16)
    up_grad = (hid_grad * swish_gate).astype(jnp.bfloat16)
    blocks = N_TENSOR
    block_width = FF // blocks
    paired = jnp.concatenate([gate_grad.reshape(TOKENS, blocks, block_width), up_grad.reshape(TOKENS, blocks, block_width)], axis=2).transpose(1, 0, 2)
    stacked = jnp.concatenate([weights[0].reshape(blocks, block_width, D), weights[1].reshape(blocks, block_width, D)], axis=1)

    def add_block(running, item_pair):
        partial_sum = scale_in * jnp.dot(item_pair[0], item_pair[1], preferred_element_type=jnp.float32)
        rounded = lax.optimization_barrier(partial_sum.astype(jnp.bfloat16))
        return (running + rounded.astype(jnp.float32), None)
    running, _ = lax.scan(add_block, jnp.zeros((TOKENS, D), jnp.float32), (paired, stacked))
    token_grad = running.astype(jnp.bfloat16)
    groups = N_DP

    def add_group(running_sum, item):
        group_tokens, group_out, group_gate, group_up, group_hidden = item
        partials = jnp.stack([contract_rows(group_gate, group_tokens), contract_rows(group_up, group_tokens), contract_rows(group_hidden, group_out)])
        rounded = lax.optimization_barrier(partials.astype(jnp.bfloat16))
        return (running_sum + rounded.astype(jnp.float32), None)
    items = (tokens.reshape(groups, TOK_GROUP, D), out_grad.reshape(groups, TOK_GROUP, D), gate_grad.reshape(groups, TOK_GROUP, FF), up_grad.reshape(groups, TOK_GROUP, FF), hidden.reshape(groups, TOK_GROUP, FF))
    sums, _ = lax.scan(add_group, jnp.zeros((3, FF, D), jnp.float32), items)
    factors = jnp.array([scale_in, scale_in, scale_out], jnp.float32)
    gradient = sums * factors[:, None, None]
    new_first = beta_first * moment_first + (1.0 - beta_first) * gradient
    new_second = beta_second * moment_second + (1.0 - beta_second) * gradient * gradient
    first_hat = new_first / (1.0 - beta_first ** step_power)
    second_hat = new_second / (1.0 - beta_second ** step_power)
    update = first_hat / (jnp.sqrt(second_hat) + epsilon) + weight_decay * master
    weight_norm = jnp.sqrt(lax.optimization_barrier(jnp.sum(master * master, axis=(1, 2))))
    update_norm = jnp.sqrt(lax.optimization_barrier(jnp.sum(update * update, axis=(1, 2))))
    trust_ratio = weight_norm / update_norm
    return (token_grad, trust_ratio[:, None, None] * update)
```

```python
import functools

import jax
import jax.numpy as jnp
from jax import lax
from jax.experimental import pallas as pl
from jax.experimental.pallas import tpu as pltpu
from jax.sharding import PartitionSpec as P

D = 5120
FF = 12800

beta_first = 0.9
beta_second = 0.95
epsilon = 1e-06
weight_decay = 0.1
step_power = 3.0

SCALE_IN = D ** (-0.5)
SCALE_OUT = FF ** (-0.5)

NY, NH, NZ, NX, NC = 4, 2, 8, 2, 2
HID = 400
COLS = 640
QUARTER = 160
GROUP = 256
TOP = 608
ROWS = 3 * HID
BF16 = jnp.bfloat16
F32 = jnp.float32
VMEM_LIMIT = 48 * 1024 * 1024

DP = [(y, h) for y in range(NY) for h in range(NH)]
TP = [(z, x, c) for z in range(NZ) for x in range(NX) for c in range(NC)]


def dp_index(y, h):
    return (y % NY) * NH + h


def tp_index(z, x, c):
    return ((z % NZ) * NX + x) * NC + c


def y_shift(k):
    return [(dp_index(y, h), dp_index(y + k, h)) for y, h in DP]


def z_shift(k):
    return [(tp_index(z, x, c), tp_index(z + k, x, c)) for z, x, c in TP]


H_SWAP = [(dp_index(y, h), dp_index(y, 1 - h)) for y, h in DP]
X_SWAP = [(tp_index(z, x, c), tp_index(z, 1 - x, c)) for z, x, c in TP]
C_SWAP = [(tp_index(z, x, c), tp_index(z, x, 1 - c)) for z, x, c in TP]
TURN = [
    (dp_index(y, h) * 32 + tp_index(z, x, c), z * 32 + tp_index(dp_index(y, h), x, c))
    for y, h in DP
    for z, x, c in TP
]

VMEM = pl.BlockSpec(memory_space=pltpu.VMEM)
SMEM = pl.BlockSpec(memory_space=pltpu.SMEM)


def dot(a, b):
    return lax.dot_general(a, b, (((1,), (0,)), ((), ())), preferred_element_type=F32)


def dot_lanes(a, b):
    return lax.dot_general(a, b, (((1,), (1,)), ((), ())), preferred_element_type=F32)


def other_if(j, x):
    return 1 - x if j else x


def lanes_of(slot):
    return pl.ds(pl.multiple_of(slot * GROUP, GROUP), GROUP)


def rows_of(quarter):
    return pl.ds(pl.multiple_of(quarter * QUARTER, QUARTER), QUARTER)


def pre_kernel(pos, m0, m1, m2, m3, o0, o1, o2, o3, wgu, wd, tk, og, own, plus, minus, far_top, far_low):
    y, x, c = pos[0], pos[2], pos[3]
    for s, (mine, other) in enumerate(((m0, o0), (m1, o1), (m2, o2), (m3, o3))):
        lanes = slice(s * GROUP, (s + 1) * GROUP)
        for ref, core in ((mine, c), (other, 1 - c)):
            for j in range(2):
                rows = rows_of(other_if(j, x) * 2 + core)
                base = j * 2 * QUARTER
                tk[rows, lanes] = ref[base : base + QUARTER, :]
                og[rows, lanes] = ref[base + QUARTER : base + 2 * QUARTER, :]
    for k in range(4):
        lanes = lanes_of(lax.rem(y + k, 4))
        both = SCALE_IN * dot(wgu[...], tk[:, lanes])
        hid = SCALE_OUT * dot(wd[...], og[:, lanes])
        if k == 2:
            far_top[...] = both[:TOP].astype(BF16)
            far_low[: 2 * HID - TOP, :] = both[TOP:].astype(BF16)
            far_low[2 * HID - TOP :, :] = hid.astype(BF16)
        else:
            out = (own, plus, None, minus)[k]
            out[: 2 * HID, :] = both.astype(out.dtype)
            out[2 * HID :, :] = hid.astype(out.dtype)


def pre_call(pos, mine, other, wgu, wd):
    sds = jax.ShapeDtypeStruct
    return pl.pallas_call(
        pre_kernel,
        out_shape=(
            sds((COLS, 4 * GROUP), BF16),
            sds((COLS, 4 * GROUP), BF16),
            sds((ROWS, GROUP), F32),
            sds((ROWS, GROUP), BF16),
            sds((ROWS, GROUP), BF16),
            sds((TOP, GROUP), BF16),
            sds((ROWS - TOP, GROUP), BF16),
        ),
        in_specs=[SMEM] + [VMEM] * 10,
        out_specs=(VMEM,) * 7,
        compiler_params=pltpu.CompilerParams(vmem_limit_bytes=VMEM_LIMIT),
        cost_estimate=pl.CostEstimate(flops=2 * ROWS * COLS * 1024, bytes_accessed=9 << 20, transcendentals=0),
        name="pre",
    )(pos, *mine, *other, wgu, wd)


def act_kernel(keep, recv, out):
    gate = keep[:HID, :] + recv[:HID, :].astype(F32)
    up = keep[HID : 2 * HID, :] + recv[HID : 2 * HID, :].astype(F32)
    hid = keep[2 * HID :, :] + recv[2 * HID :, :].astype(F32)
    sig = jax.nn.sigmoid(gate)
    swish = gate * sig
    out[:HID, :] = (hid * up * sig * (1.0 + gate * (1.0 - sig))).astype(BF16)
    out[HID : 2 * HID, :] = (hid * swish).astype(BF16)
    out[2 * HID :, :] = (swish * up).astype(BF16)


def act_call(keep, recv):
    return pl.pallas_call(
        act_kernel,
        out_shape=jax.ShapeDtypeStruct((ROWS, GROUP // 2), BF16),
        in_specs=[VMEM] * 2,
        out_specs=VMEM,
        compiler_params=pltpu.CompilerParams(vmem_limit_bytes=VMEM_LIMIT),
        cost_estimate=pl.CostEstimate(flops=HID * 128 * 20, bytes_accessed=2 << 20, transcendentals=HID * 128),
        name="act",
    )(keep, recv)


def token_kernel(pos, own, before, after, far_top, far_low, wt, grads, send, keep, full):
    y, x, c = pos[0], pos[2], pos[3]
    grads[:, lanes_of(y)] = own[...]
    grads[:, lanes_of(lax.rem(y + 3, 4))] = before[...]
    grads[:, lanes_of(lax.rem(y + 1, 4))] = after[...]
    far = lanes_of(lax.rem(y + 2, 4))
    grads[:TOP, far] = far_top[...]
    grads[TOP:, far] = far_low[...]
    for s in range(4):
        full[...] = SCALE_IN * dot(wt[...], grads[: 2 * HID, s * GROUP : (s + 1) * GROUP])
        for j in range(2):
            rows = slice(j * QUARTER, (j + 1) * QUARTER)
            send[s, rows, :] = full[rows_of(other_if(j, x) * 2 + 1 - c), :].astype(BF16)
            keep[s, rows, :] = full[rows_of(other_if(j, x) * 2 + c), :].astype(BF16)


def token_call(pos, parts, wt):
    sds = jax.ShapeDtypeStruct
    return pl.pallas_call(
        token_kernel,
        out_shape=(
            sds((ROWS, 4 * GROUP), BF16),
            sds((4, 2 * QUARTER, GROUP), BF16),
            sds((4, 2 * QUARTER, GROUP), BF16),
        ),
        in_specs=[SMEM] + [VMEM] * 6,
        out_specs=(VMEM,) * 3,
        scratch_shapes=[pltpu.VMEM((COLS, GROUP), F32)],
        compiler_params=pltpu.CompilerParams(vmem_limit_bytes=VMEM_LIMIT),
        cost_estimate=pl.CostEstimate(flops=2 * 800 * COLS * 1024, bytes_accessed=9 << 20, transcendentals=0),
        name="token",
    )(pos, *parts, wt)


def weight_kernel(g, tk, og, out):
    m = pl.program_id(0)

    @pl.when(m < 2)
    def _():
        out[0] = dot_lanes(g[...], tk[...])

    @pl.when(m == 2)
    def _():
        out[0] = dot_lanes(g[...], og[...])


def weight_call(grads, tk, og):
    return pl.pallas_call(
        weight_kernel,
        out_shape=jax.ShapeDtypeStruct((3, HID, COLS), F32),
        grid=(3, 5),
        in_specs=[
            pl.BlockSpec((HID, 1024), lambda m, n: (m, 0)),
            pl.BlockSpec((128, 1024), lambda m, n: (n, 0)),
            pl.BlockSpec((128, 1024), lambda m, n: (n, 0)),
        ],
        out_specs=pl.BlockSpec((1, HID, 128), lambda m, n: (m, 0, n)),
        compiler_params=pltpu.CompilerParams(vmem_limit_bytes=VMEM_LIMIT),
        cost_estimate=pl.CostEstimate(flops=2 * ROWS * COLS * 1024, bytes_accessed=9 << 20, transcendentals=0),
        name="weight",
    )(grads, tk, og)


def step_kernel(g, tk, og, first_sum, master, m1, m2, update, squares, total):
    m = pl.program_id(0)
    n = pl.program_id(1)

    @pl.when(m < 2)
    def _():
        total[...] = SCALE_IN * (first_sum[0] + dot_lanes(g[...], tk[...]))

    @pl.when(m == 2)
    def _():
        total[...] = SCALE_OUT * (first_sum[0] + dot_lanes(g[...], og[...]))

    gradient = total[...]
    weights = master[0]
    new_first = beta_first * m1[0] + (1.0 - beta_first) * gradient
    new_second = beta_second * m2[0] + (1.0 - beta_second) * gradient * gradient
    first_hat = new_first / (1.0 - beta_first**step_power)
    second_hat = new_second / (1.0 - beta_second**step_power)
    result = first_hat / (jnp.sqrt(second_hat) + epsilon) + weight_decay * weights
    update[0] = result
    weight_part = jnp.sum((weights * weights).reshape(HID // 8, 8, 128), axis=0)
    update_part = jnp.sum((result * result).reshape(HID // 8, 8, 128), axis=0)

    @pl.when(n == 0)
    def _():
        squares[0, 0] = weight_part
        squares[0, 1] = update_part

    @pl.when(n > 0)
    def _():
        squares[0, 0] += weight_part
        squares[0, 1] += update_part


def step_call(grads, tk, og, first_sum, master, m1, m2):
    sds = jax.ShapeDtypeStruct
    state = pl.BlockSpec((1, HID, 128), lambda m, n: (m, 0, n))
    return pl.pallas_call(
        step_kernel,
        out_shape=(sds((3, HID, COLS), F32), sds((3, 2, 8, 128), F32)),
        grid=(3, 5),
        in_specs=[
            pl.BlockSpec((HID, 1024), lambda m, n: (m, 0)),
            pl.BlockSpec((128, 1024), lambda m, n: (n, 0)),
            pl.BlockSpec((128, 1024), lambda m, n: (n, 0)),
            state,
            state,
            state,
            state,
        ],
        out_specs=(state, pl.BlockSpec((1, 2, 8, 128), lambda m, n: (m, 0, 0, 0))),
        scratch_shapes=[pltpu.VMEM((HID, 128), F32)],
        compiler_params=pltpu.CompilerParams(vmem_limit_bytes=VMEM_LIMIT),
        cost_estimate=pl.CostEstimate(flops=2 * ROWS * COLS * 1024, bytes_accessed=19 << 20, transcendentals=0),
        name="step",
    )(grads, tk, og, first_sum, master, m1, m2)


def add_over(value, axis, count):
    sent = jnp.broadcast_to(value[None], (count,) + value.shape)
    return jnp.sum(lax.all_to_all(sent, axis, 0, 0), axis=0)


def z_send(value, k):
    return lax.ppermute(value, "tensor", z_shift(k))


def local(tokens, out_grad, master, moment_first, moment_second):
    dp = lax.axis_index("dp")
    tensor = lax.axis_index("tensor")
    h = dp % 2
    pos = jnp.stack([dp // 2, h, (tensor // 2) % 2, tensor % 2]).astype(jnp.int32)

    piece = jnp.concatenate([tokens.T, out_grad.T], axis=0)
    piece = lax.ppermute(piece, ("dp", "tensor"), TURN)
    held = jnp.concatenate([piece, lax.ppermute(piece, "tensor", X_SWAP)], axis=0)

    weights = master.astype(BF16)
    wgu = weights[:2].reshape(2 * HID, COLS)
    wd = weights[2]
    wt = wgu.T

    up1, down1 = z_send(held, 1), z_send(held, -1)
    up2, down2 = z_send(up1, 1), z_send(down1, -1)
    up3, down3 = z_send(up2, 1), z_send(down2, -1)
    half = 2 * QUARTER
    across = jnp.concatenate([z_send(up3[:half], 1), z_send(down3[half:], -1)], axis=0)
    chunks = (
        ((0, 1, -1, 2), (held, down1, up1, down2)),
        ((-2, 3, -3, 4), (up2, down3, up3, across)),
    )

    def swap_core(value):
        return lax.ppermute(value, "tensor", C_SWAP)

    def scatter(mine):
        other = [swap_core(v) for v in mine]
        tk, og, own, plus, minus, far_top, far_low = pre_call(pos, mine, other, wgu, wd)
        got_top = lax.ppermute(far_top, "dp", y_shift(1))
        got_low = lax.ppermute(far_low, "dp", y_shift(-1))
        plus = plus.at[:TOP].set((plus[:TOP].astype(F32) + got_top.astype(F32)).astype(BF16))
        minus = minus.at[TOP:].set((minus[TOP:].astype(F32) + got_low.astype(F32)).astype(BF16))
        from_below = lax.ppermute(plus, "dp", y_shift(1))
        from_above = lax.ppermute(minus, "dp", y_shift(-1))
        total = own + from_below.astype(F32) + from_above.astype(F32)
        left, right = total[:, : GROUP // 2], total[:, GROUP // 2 :]
        keep = jnp.where(h == 0, left, right)
        send = jnp.where(h == 0, right, left).astype(BF16)
        return tk, og, keep, lax.ppermute(send, "dp", H_SWAP)

    def gather(keep, recv):
        mine = act_call(keep, recv)
        other = lax.ppermute(mine, "dp", H_SWAP)
        block = jnp.where(
            h == 0, jnp.concatenate([mine, other], axis=1), jnp.concatenate([other, mine], axis=1)
        )
        before = lax.ppermute(block, "dp", y_shift(1))
        after = lax.ppermute(block, "dp", y_shift(-1))
        far_top = lax.ppermute(before[:TOP], "dp", y_shift(1))
        far_low = lax.ppermute(after[TOP:], "dp", y_shift(-1))
        return block, before, after, far_top, far_low

    def token_part(parts):
        grads, send, keep = token_call(pos, parts, wt)
        part = keep.astype(F32) + swap_core(send).astype(F32)
        got = lax.ppermute(part[:, QUARTER:].astype(BF16), "tensor", X_SWAP)
        return grads, part[:, :QUARTER] + got.astype(F32)

    tk1, og1, keep1, recv1 = scatter(chunks[0][1])
    tk2, og2, keep2, recv2 = scatter(chunks[1][1])
    parts1 = gather(keep1, recv1)
    parts2 = gather(keep2, recv2)
    grads1, sum1 = token_part(parts1)
    first_sum = weight_call(grads1, tk1, og1)
    grads2, sum2 = token_part(parts2)

    total = sum1[0]
    for offsets, part in ((chunks[0][0], sum1), (chunks[1][0], sum2)):
        for s, k in enumerate(offsets):
            if k != 0:
                total = total + z_send(part[s].astype(BF16), k).astype(F32)
    token_grad = lax.ppermute(total.astype(BF16), ("dp", "tensor"), TURN).T

    update, squares = step_call(grads2, tk2, og2, first_sum, master, moment_first, moment_second)
    sums = jnp.sum(squares, axis=(2, 3)).reshape(1, 6)
    sums = jnp.broadcast_to(jnp.pad(sums, ((0, 0), (0, 122))), (8, 128))
    sums = add_over(add_over(sums, "tensor", 32), "dp", 8)[0, :6].reshape(3, 2)
    trust_ratio = jnp.sqrt(sums[:, 0]) / jnp.sqrt(sums[:, 1])
    return (token_grad, trust_ratio[:, None, None] * update)


def solution(mesh):
    state = P(None, "tensor", "dp")
    rows = P("dp", "tensor")
    return jax.shard_map(
        local,
        mesh=mesh,
        in_specs=(rows, rows, state, state, state),
        out_specs=(rows, state),
        check_vma=False,
    )
```

```python
import functools

import jax
import jax.numpy as jnp
from jax import lax
from jax.experimental import pallas as pl
from jax.experimental.pallas import tpu as pltpu
from jax.sharding import PartitionSpec as P

D = 5120
FF = 12800

beta_first = 0.9
beta_second = 0.95
epsilon = 1e-06
weight_decay = 0.1
step_power = 3.0

SCALE_IN = D ** (-0.5)
SCALE_OUT = FF ** (-0.5)

NY, NH, NZ, NX, NC = 4, 2, 8, 2, 2
HID = 400
COLS = 640
QUARTER = 160
GROUP = 256
TOP = 608
ROWS = 3 * HID
BF16 = jnp.bfloat16
F32 = jnp.float32
MIB = 1 << 20

DP = [(y, h) for y in range(NY) for h in range(NH)]
TP = [(z, x, c) for z in range(NZ) for x in range(NX) for c in range(NC)]


def dp_index(y, h):
    return (y % NY) * NH + h


def tp_index(z, x, c):
    return ((z % NZ) * NX + x) * NC + c


def y_shift(k):
    return [(dp_index(y, h), dp_index(y + k, h)) for y, h in DP]


def z_shift(k):
    return [(tp_index(z, x, c), tp_index(z + k, x, c)) for z, x, c in TP]


H_SWAP = [(dp_index(y, h), dp_index(y, 1 - h)) for y, h in DP]
X_SWAP = [(tp_index(z, x, c), tp_index(z, 1 - x, c)) for z, x, c in TP]
C_SWAP = [(tp_index(z, x, c), tp_index(z, x, 1 - c)) for z, x, c in TP]
TURN = [
    (dp_index(y, h) * 32 + tp_index(z, x, c), z * 32 + tp_index(dp_index(y, h), x, c))
    for y, h in DP
    for z, x, c in TP
]

VMEM = pl.BlockSpec(memory_space=pltpu.VMEM)
SMEM = pl.BlockSpec(memory_space=pltpu.SMEM)


def dot(a, b):
    return lax.dot_general(a, b, (((1,), (0,)), ((), ())), preferred_element_type=F32)


def dot_lanes(a, b):
    return lax.dot_general(a, b, (((1,), (1,)), ((), ())), preferred_element_type=F32)


def other_if(j, x):
    return 1 - x if j else x


def lanes_of(slot):
    return pl.ds(pl.multiple_of(slot * GROUP, GROUP), GROUP)


def rows_of(quarter):
    return pl.ds(pl.multiple_of(quarter * QUARTER, QUARTER), QUARTER)


def after(value, *earlier):
    return lax.optimization_barrier((value,) + earlier)[0]


def call(kernel, name, limit, flops, read, out_shape, args, **kw):
    kw.setdefault("in_specs", [VMEM] * len(args))
    kw.setdefault("out_specs", jax.tree.map(lambda _: VMEM, out_shape))
    return pl.pallas_call(
        kernel,
        out_shape=out_shape,
        compiler_params=pltpu.CompilerParams(vmem_limit_bytes=limit * MIB),
        cost_estimate=pl.CostEstimate(flops=flops, bytes_accessed=read, transcendentals=0),
        name=name,
        **kw,
    )(*args)


def sds(shape, dtype):
    return jax.ShapeDtypeStruct(shape, dtype)


def fold(values):
    return jnp.sum(values.reshape(-1, 8, COLS), axis=0)


def cast_kernel(master, wgu, wd, wt, squares):
    m = pl.program_id(0)
    values = master[0]
    weights = values.astype(BF16)
    squares[0] = fold(values * values)

    @pl.when(m < 2)
    def _():
        wgu[0] = weights
        wt[0] = weights.T

    @pl.when(m == 2)
    def _():
        wd[...] = weights


def cast_call(master):
    clamp = lambda m: (jnp.minimum(m, 1), 0, 0)
    return call(
        cast_kernel,
        "cast",
        14,
        1 << 20,
        6 << 20,
        (sds((2, HID, COLS), BF16), sds((HID, COLS), BF16), sds((2, COLS, HID), BF16), sds((3, 8, COLS), F32)),
        (master,),
        grid=(3,),
        in_specs=[pl.BlockSpec((1, HID, COLS), lambda m: (m, 0, 0))],
        out_specs=(
            pl.BlockSpec((1, HID, COLS), clamp),
            pl.BlockSpec((HID, COLS), lambda m: (0, 0)),
            pl.BlockSpec((1, COLS, HID), clamp),
            pl.BlockSpec((1, 8, COLS), lambda m: (m, 0, 0)),
        ),
    )


def pre_kernel(pos, m0, m1, m2, m3, o0, o1, o2, o3, wgu, wd, tk, og, own, plus, minus, far_top, far_low):
    y, x, c = pos[0], pos[2], pos[3]
    for s, (mine, other) in enumerate(((m0, o0), (m1, o1), (m2, o2), (m3, o3))):
        lanes = lanes_of(lax.rem(s + 4 - y, 4))
        for ref, core in ((mine, c), (other, 1 - c)):
            for j in range(2):
                rows = rows_of(other_if(j, x) * 2 + core)
                base = j * 2 * QUARTER
                tk[rows, lanes] = ref[base : base + QUARTER, :]
                og[rows, lanes] = ref[base + QUARTER : base + 2 * QUARTER, :]
    for k in (2, 1, 3, 0):
        lanes = slice(k * GROUP, (k + 1) * GROUP)
        gate = SCALE_IN * dot(wgu[0], tk[:, lanes])
        up = SCALE_IN * dot(wgu[1], tk[:, lanes])
        hid = SCALE_OUT * dot(wd[...], og[:, lanes])
        if k == 2:
            far_top[:HID, :] = gate.astype(BF16)
            far_top[HID:, :] = up[: TOP - HID].astype(BF16)
            far_low[: 2 * HID - TOP, :] = up[TOP - HID :].astype(BF16)
            far_low[2 * HID - TOP :, :] = hid.astype(BF16)
        else:
            out = (own, plus, None, minus)[k]
            out[:HID, :] = gate.astype(out.dtype)
            out[HID : 2 * HID, :] = up.astype(out.dtype)
            out[2 * HID :, :] = hid.astype(out.dtype)


def pre_call(pos, mine, other, wgu, wd):
    return call(
        pre_kernel,
        "pre",
        14,
        2 * ROWS * COLS * 1024,
        9 << 20,
        (
            sds((COLS, 4 * GROUP), BF16),
            sds((COLS, 4 * GROUP), BF16),
            sds((ROWS, GROUP), F32),
            sds((ROWS, GROUP), BF16),
            sds((ROWS, GROUP), BF16),
            sds((TOP, GROUP), BF16),
            sds((ROWS - TOP, GROUP), BF16),
        ),
        (pos, *mine, *other, wgu, wd),
        in_specs=[SMEM] + [VMEM] * 10,
    )


def act_kernel(keep, recv, out):
    gate = keep[:HID, :] + recv[:HID, :].astype(F32)
    up = keep[HID : 2 * HID, :] + recv[HID : 2 * HID, :].astype(F32)
    hid = keep[2 * HID :, :] + recv[2 * HID :, :].astype(F32)
    sig = jax.nn.sigmoid(gate)
    swish = gate * sig
    out[:HID, :] = (hid * up * sig * (1.0 + gate * (1.0 - sig))).astype(BF16)
    out[HID : 2 * HID, :] = (hid * swish).astype(BF16)
    out[2 * HID :, :] = (swish * up).astype(BF16)


def act_call(keep, recv):
    return call(act_kernel, "act", 6, HID * 128 * 40, 2 << 20, sds((ROWS, GROUP // 2), BF16), (keep, recv))


def token_kernel(count, split, pos, *refs):
    parts, (wt, send, keep, full) = refs[:-4], refs[-4:]
    x, c = pos[2], pos[3]
    for s in range(count):
        if s == split:
            top, low = parts[s], parts[s + 1]
            gate, up0, up1 = top[:HID, :], top[HID:, :], low[: 2 * HID - TOP, :]
            up = jnp.concatenate([up0, up1], axis=0)
        else:
            part = parts[s if split is None or s < split else s + 1]
            gate, up = part[:HID, :], part[HID : 2 * HID, :]
        full[...] = SCALE_IN * (dot(wt[0], gate) + dot(wt[1], up))
        for j in range(2):
            rows = slice(j * QUARTER, (j + 1) * QUARTER)
            send[s, rows, :] = full[rows_of(other_if(j, x) * 2 + 1 - c), :].astype(BF16)
            keep[s, rows, :] = full[rows_of(other_if(j, x) * 2 + c), :].astype(BF16)


def token_call(pos, parts, wt, split):
    count = len(parts) - (split is not None)
    shape = sds((count, 2 * QUARTER, GROUP), BF16)
    return call(
        functools.partial(token_kernel, count, split),
        "token",
        10,
        2 * 800 * COLS * GROUP * count,
        9 << 20,
        (shape, shape),
        (pos, *parts, wt),
        in_specs=[SMEM] + [VMEM] * (len(parts) + 1),
        scratch_shapes=[pltpu.VMEM((COLS, GROUP), F32)],
    )


def lay(own, before, after_, far_top, far_low, grads):
    grads[:, :GROUP] = own[...]
    grads[:, GROUP : 2 * GROUP] = after_[...]
    grads[:TOP, 2 * GROUP : 3 * GROUP] = far_top[...]
    grads[TOP:, 2 * GROUP : 3 * GROUP] = far_low[...]
    grads[:, 3 * GROUP :] = before[...]


def weight_kernel(own, before, after_, far_top, far_low, tk, og, out, grads):
    lay(own, before, after_, far_top, far_low, grads)
    out[0] = dot_lanes(grads[:HID, :], tk[...])
    out[1] = dot_lanes(grads[HID : 2 * HID, :], tk[...])
    out[2] = dot_lanes(grads[2 * HID :, :], og[...])


def weight_call(parts, tk, og):
    return call(
        weight_kernel,
        "weight",
        18,
        2 * ROWS * COLS * 1024,
        9 << 20,
        sds((3, HID, COLS), F32),
        (*parts, tk, og),
        scratch_shapes=[pltpu.VMEM((ROWS, 4 * GROUP), BF16)],
    )


def more_kernel(own, before, after_, tk, og, first_sum, out, grads):
    grads[:, :GROUP] = own[...]
    grads[:, GROUP : 2 * GROUP] = after_[...]
    grads[:, 2 * GROUP :] = before[...]
    for i, ref in enumerate((tk, tk, og)):
        rows = slice(i * HID, (i + 1) * HID)
        part = dot_lanes(grads[rows, : 2 * GROUP], ref[:, : 2 * GROUP])
        part += dot_lanes(grads[rows, 2 * GROUP :], ref[:, 3 * GROUP :])
        out[i] = first_sum[i] + part


def more_call(own, before, after_, tk, og, first_sum):
    return call(
        more_kernel,
        "more",
        20,
        2 * ROWS * COLS * 768,
        12 << 20,
        sds((3, HID, COLS), F32),
        (own, before, after_, tk, og, first_sum),
        scratch_shapes=[pltpu.VMEM((ROWS, 3 * GROUP), BF16)],
    )


BLOCK = 40


def step_kernel(far_top, far_low, tk, og, first_sum, master, m1, m2, update, squares, total):
    lanes = slice(2 * GROUP, 3 * GROUP)
    up = jnp.concatenate([far_top[HID:, :], far_low[: 2 * HID - TOP, :]], axis=0)
    for i, (part, ref) in enumerate(((far_top[:HID, :], tk), (up, tk), (far_low[2 * HID - TOP :, :], og))):
        scale = SCALE_OUT if i == 2 else SCALE_IN
        total[...] = dot_lanes(part, ref[:, lanes])

        def block(n, running):
            rows = pl.ds(pl.multiple_of(n * BLOCK, 8), BLOCK)
            gradient = scale * (first_sum[i, rows, :] + total[rows, :])
            new_first = beta_first * m1[i, rows, :] + (1.0 - beta_first) * gradient
            new_second = beta_second * m2[i, rows, :] + (1.0 - beta_second) * gradient * gradient
            first_hat = new_first * (1.0 / (1.0 - beta_first**step_power))
            second_hat = new_second * (1.0 / (1.0 - beta_second**step_power))
            result = first_hat / (jnp.sqrt(second_hat) + epsilon) + weight_decay * master[i, rows, :]
            update[i, rows, :] = result
            return running + fold(result * result)

        squares[i] = lax.fori_loop(0, HID // BLOCK, block, jnp.zeros((8, COLS), F32))


def step_call(far, tk, og, first_sum, master, m1, m2):
    return call(
        step_kernel,
        "step",
        26,
        2 * ROWS * COLS * 256,
        19 << 20,
        (sds((3, HID, COLS), F32), sds((3, 8, COLS), F32)),
        (*far, tk, og, first_sum, master, m1, m2),
        scratch_shapes=[pltpu.VMEM((HID, COLS), F32)],
    )


def add_over(value, axis, count):
    sent = jnp.broadcast_to(value[None], (count,) + value.shape)
    return jnp.sum(lax.all_to_all(sent, axis, 0, 0), axis=0)


def z_send(value, k):
    return lax.ppermute(value, "tensor", z_shift(k))


NEAR = (0, 1, -1, 2)
FAR = (-2, 3, -3, 4)


def z_home(value, offsets, k):
    pairs = [
        (dp_index(y, h) * 32 + tp_index(z, x, c), dp_index(y, h) * 32 + tp_index(z + offsets[(y + k) % 4], x, c))
        for y, h in DP
        for z, x, c in TP
    ]
    return lax.ppermute(value, ("dp", "tensor"), pairs)


def local(tokens, out_grad, master, moment_first, moment_second):
    dp = lax.axis_index("dp")
    tensor = lax.axis_index("tensor")
    h = dp % 2
    pos = jnp.stack([dp // 2, h, (tensor // 2) % 2, tensor % 2]).astype(jnp.int32)
    left_half = h == 0

    piece = jnp.concatenate([after(tokens, pos, left_half).T, out_grad.T], axis=0)
    piece = lax.ppermute(piece, ("dp", "tensor"), TURN)
    wgu, wd, wt, weight_squares = cast_call(master)
    piece = after(piece, wgu, wd, wt, weight_squares)
    held = jnp.concatenate([piece, lax.ppermute(piece, "tensor", X_SWAP)], axis=0)

    up1, down1 = z_send(held, 1), z_send(held, -1)
    up2, down2 = z_send(up1, 1), z_send(down1, -1)
    up3, down3 = z_send(up2, 1), z_send(down2, -1)
    near_groups = (held, down1, up1, down2)

    def swap_core(value):
        return lax.ppermute(value, "tensor", C_SWAP)

    def pre(mine):
        other = [swap_core(v) for v in mine]
        return pre_call(pos, mine, other, wgu, wd)

    def scatter_far(far_top, far_low, plus, minus):
        got_top = lax.ppermute(far_top, "dp", y_shift(1))
        got_low = lax.ppermute(far_low, "dp", y_shift(-1))
        plus = plus.at[:TOP].set((plus[:TOP].astype(F32) + got_top.astype(F32)).astype(BF16))
        minus = minus.at[TOP:].set((minus[TOP:].astype(F32) + got_low.astype(F32)).astype(BF16))
        return plus, minus

    def scatter_near(own, plus, minus):
        from_below = lax.ppermute(plus, "dp", y_shift(1))
        from_above = lax.ppermute(minus, "dp", y_shift(-1))
        total = own + from_below.astype(F32) + from_above.astype(F32)
        left, right = total[:, : GROUP // 2], total[:, GROUP // 2 :]
        keep = jnp.where(left_half, left, right)
        send = jnp.where(left_half, right, left).astype(BF16)
        return keep, send

    def swap_h(value):
        return lax.ppermute(value, "dp", H_SWAP)

    def join(mine):
        other = swap_h(mine)
        return jnp.where(
            left_half, jnp.concatenate([mine, other], axis=1), jnp.concatenate([other, mine], axis=1)
        )

    def gather_near(block):
        return lax.ppermute(block, "dp", y_shift(1)), lax.ppermute(block, "dp", y_shift(-1))

    def gather_far(before, after_):
        return (
            lax.ppermute(before[:TOP], "dp", y_shift(1)),
            lax.ppermute(after_[TOP:], "dp", y_shift(-1)),
        )

    def token_part(parts, split=None):
        send, keep = token_call(pos, parts, wt, split)
        part = keep.astype(F32) + swap_core(send).astype(F32)
        got = lax.ppermute(part[:, QUARTER:].astype(BF16), "tensor", X_SWAP)
        return (part[:, :QUARTER] + got.astype(F32)).astype(BF16)

    def token_sum(part, homes):
        got = [z_home(part[i], offsets, k) for i, (offsets, k) in enumerate(homes)]
        return sum(v.astype(F32) for v in got)

    tk1, og1, own1, plus1, minus1, far_top1, far_low1 = pre(near_groups)
    up3, down3 = after(up3, far_top1), after(down3, far_top1)
    half = 2 * QUARTER
    across = jnp.concatenate([z_send(up3[:half], 1), z_send(down3[half:], -1)], axis=0)
    plus1, minus1 = scatter_far(far_top1, far_low1, plus1, minus1)
    across = after(across, plus1, minus1)
    tk2, og2, own2, plus2, minus2, far_top2, far_low2 = pre((up2, down3, up3, across))
    keep1, send1 = scatter_near(own1, plus1, minus1)
    plus2, minus2 = scatter_far(far_top2, far_low2, plus2, minus2)
    keep2, send2 = scatter_near(own2, plus2, minus2)
    block1 = join(act_call(keep1, swap_h(send1)))
    send2 = after(send2, block1)
    before1, after1 = gather_near(block1)
    block2 = join(act_call(keep2, swap_h(send2)))
    far1 = gather_far(before1, after1)
    before2, after2 = gather_near(block2)

    early = token_part((block1, after1, before1, *far1), 3)
    early = token_sum(early, ((NEAR, 0), (NEAR, 1), (NEAR, 3), (NEAR, 2)))
    first_sum = weight_call((block1, before1, after1, *far1), tk1, og1)
    far2 = gather_far(before2, after2)
    beside = token_part((block2, after2, before2))
    beside = token_sum(beside, ((FAR, 0), (FAR, 1), (FAR, 3)))
    first_sum = more_call(block2, before2, after2, tk2, og2, first_sum)
    far2 = tuple(after(v, first_sum) for v in far2)
    last = token_sum(token_part(far2, 0), ((FAR, 2),))
    token_grad = lax.ppermute((early + beside + last).astype(BF16), ("dp", "tensor"), TURN).T

    first_sum = after(first_sum, early)
    update, squares = step_call(far2, tk2, og2, first_sum, master, moment_first, moment_second)
    sums = jnp.sum(jnp.stack([weight_squares, squares]), axis=(2, 3)).reshape(1, 6)
    sums = jnp.broadcast_to(jnp.pad(sums, ((0, 0), (0, 122))), (8, 128))
    sums = after(add_over(sums, "tensor", 32), beside)
    sums = add_over(sums, "dp", 8)[0, :6].reshape(2, 3)
    trust_ratio = jnp.sqrt(sums[0]) / jnp.sqrt(sums[1])
    return (token_grad, trust_ratio[:, None, None] * update)


def solution(mesh):
    state = P(None, "tensor", "dp")
    rows = P("dp", "tensor")
    return jax.shard_map(
        local,
        mesh=mesh,
        in_specs=(rows, rows, state, state, state),
        out_specs=(rows, state),
        check_vma=False,
    )
```

```python
import functools

import jax
import jax.numpy as jnp
from jax import lax
from jax.experimental import pallas as pl
from jax.experimental.pallas import tpu as pltpu
from jax.sharding import PartitionSpec as P

D = 5120
FF = 12800

beta_first = 0.9
beta_second = 0.95
epsilon = 1e-06
weight_decay = 0.1
step_power = 3.0

SCALE_IN = D ** (-0.5)
SCALE_OUT = FF ** (-0.5)

NY, NH, NZ, NX, NC = 4, 2, 8, 2, 2
HID = 400
COLS = 640
QUARTER = 160
GROUP = 256
TOP = 608
ROWS = 3 * HID
BF16 = jnp.bfloat16
F32 = jnp.float32
MIB = 1 << 20

DP = [(y, h) for y in range(NY) for h in range(NH)]
TP = [(z, x, c) for z in range(NZ) for x in range(NX) for c in range(NC)]


def dp_index(y, h):
    return (y % NY) * NH + h


def tp_index(z, x, c):
    return ((z % NZ) * NX + x) * NC + c


def y_shift(k):
    return [(dp_index(y, h), dp_index(y + k, h)) for y, h in DP]


def z_shift(k):
    return [(tp_index(z, x, c), tp_index(z + k, x, c)) for z, x, c in TP]


H_SWAP = [(dp_index(y, h), dp_index(y, 1 - h)) for y, h in DP]
X_SWAP = [(tp_index(z, x, c), tp_index(z, 1 - x, c)) for z, x, c in TP]
C_SWAP = [(tp_index(z, x, c), tp_index(z, x, 1 - c)) for z, x, c in TP]
TURN = [
    (dp_index(y, h) * 32 + tp_index(z, x, c), z * 32 + tp_index(dp_index(y, h), x, c))
    for y, h in DP
    for z, x, c in TP
]

VMEM = pl.BlockSpec(memory_space=pltpu.VMEM)
SMEM = pl.BlockSpec(memory_space=pltpu.SMEM)


def dot(a, b):
    return lax.dot_general(a, b, (((1,), (0,)), ((), ())), preferred_element_type=F32)


def dot_lanes(a, b):
    return lax.dot_general(a, b, (((1,), (1,)), ((), ())), preferred_element_type=F32)


def other_if(j, x):
    return 1 - x if j else x


def lanes_of(slot):
    return pl.ds(pl.multiple_of(slot * GROUP, GROUP), GROUP)


def rows_of(quarter):
    return pl.ds(pl.multiple_of(quarter * QUARTER, QUARTER), QUARTER)


def after(value, *earlier):
    return lax.optimization_barrier((value,) + earlier)[0]


def call(kernel, name, limit, flops, read, out_shape, args, deps=(), **kw):
    count = len(args)

    def body(*refs):
        kernel(*refs[:count], *refs[count + len(deps) :])

    specs = kw.pop("in_specs", [VMEM] * count) + [pl.BlockSpec(memory_space=pl.ANY)] * len(deps)
    kw.setdefault("out_specs", jax.tree.map(lambda _: VMEM, out_shape))
    return pl.pallas_call(
        body,
        out_shape=out_shape,
        in_specs=specs,
        compiler_params=pltpu.CompilerParams(vmem_limit_bytes=limit * MIB),
        cost_estimate=pl.CostEstimate(flops=flops, bytes_accessed=read, transcendentals=0),
        name=name,
        **kw,
    )(*args, *deps)


def sds(shape, dtype):
    return jax.ShapeDtypeStruct(shape, dtype)


def fold(values):
    return jnp.sum(values.reshape(-1, 8, COLS), axis=0)


def cast_kernel(master, wgu, wd, wt, squares):
    m = pl.program_id(0)
    values = master[0]
    weights = values.astype(BF16)
    squares[0] = fold(values * values)

    @pl.when(m < 2)
    def _():
        wgu[0] = weights
        wt[0] = weights.T

    @pl.when(m == 2)
    def _():
        wd[...] = weights


def cast_call(master):
    clamp = lambda m: (jnp.minimum(m, 1), 0, 0)
    return call(
        cast_kernel,
        "cast",
        14,
        1 << 20,
        6 << 20,
        (sds((2, HID, COLS), BF16), sds((HID, COLS), BF16), sds((2, COLS, HID), BF16), sds((3, 8, COLS), F32)),
        (master,),
        grid=(3,),
        in_specs=[pl.BlockSpec((1, HID, COLS), lambda m: (m, 0, 0))],
        out_specs=(
            pl.BlockSpec((1, HID, COLS), clamp),
            pl.BlockSpec((HID, COLS), lambda m: (0, 0)),
            pl.BlockSpec((1, COLS, HID), clamp),
            pl.BlockSpec((1, 8, COLS), lambda m: (m, 0, 0)),
        ),
    )


def pre_kernel(pos, m0, m1, m2, m3, o0, o1, o2, o3, wgu, wd, tk, og, own, plus, minus, far_top, far_low):
    y, x, c = pos[0], pos[2], pos[3]
    for s, (mine, other) in enumerate(((m0, o0), (m1, o1), (m2, o2), (m3, o3))):
        lanes = lanes_of(lax.rem(s + 4 - y, 4))
        for ref, core in ((mine, c), (other, 1 - c)):
            for j in range(2):
                rows = rows_of(other_if(j, x) * 2 + core)
                base = j * 2 * QUARTER
                tk[rows, lanes] = ref[base : base + QUARTER, :]
                og[rows, lanes] = ref[base + QUARTER : base + 2 * QUARTER, :]
    for k in (2, 1, 3, 0):
        lanes = slice(k * GROUP, (k + 1) * GROUP)
        gate = SCALE_IN * dot(wgu[0], tk[:, lanes])
        up = SCALE_IN * dot(wgu[1], tk[:, lanes])
        hid = SCALE_OUT * dot(wd[...], og[:, lanes])
        if k == 2:
            far_top[:HID, :] = gate.astype(BF16)
            far_top[HID:, :] = up[: TOP - HID].astype(BF16)
            far_low[: 2 * HID - TOP, :] = up[TOP - HID :].astype(BF16)
            far_low[2 * HID - TOP :, :] = hid.astype(BF16)
        else:
            out = (own, plus, None, minus)[k]
            out[:HID, :] = gate.astype(out.dtype)
            out[HID : 2 * HID, :] = up.astype(out.dtype)
            out[2 * HID :, :] = hid.astype(out.dtype)


def pre_call(pos, mine, other, wgu, wd):
    return call(
        pre_kernel,
        "pre",
        14,
        2 * ROWS * COLS * 1024,
        9 << 20,
        (
            sds((COLS, 4 * GROUP), BF16),
            sds((COLS, 4 * GROUP), BF16),
            sds((ROWS, GROUP), F32),
            sds((ROWS, GROUP), BF16),
            sds((ROWS, GROUP), BF16),
            sds((TOP, GROUP), BF16),
            sds((ROWS - TOP, GROUP), BF16),
        ),
        (pos, *mine, *other, wgu, wd),
        in_specs=[SMEM] + [VMEM] * 10,
    )


def act_kernel(keep, recv, out):
    gate = keep[:HID, :] + recv[:HID, :].astype(F32)
    up = keep[HID : 2 * HID, :] + recv[HID : 2 * HID, :].astype(F32)
    hid = keep[2 * HID :, :] + recv[2 * HID :, :].astype(F32)
    sig = jax.nn.sigmoid(gate)
    swish = gate * sig
    out[:HID, :] = (hid * up * sig * (1.0 + gate * (1.0 - sig))).astype(BF16)
    out[HID : 2 * HID, :] = (hid * swish).astype(BF16)
    out[2 * HID :, :] = (swish * up).astype(BF16)


def act_call(keep, recv):
    return call(act_kernel, "act", 6, HID * 128 * 40, 2 << 20, sds((ROWS, GROUP // 2), BF16), (keep, recv))


def token_kernel(count, split, pos, *refs):
    parts, (wt, send, keep, full) = refs[:-4], refs[-4:]
    x, c = pos[2], pos[3]
    for s in range(count):
        if s == split:
            top, low = parts[s], parts[s + 1]
            gate, up0, up1 = top[:HID, :], top[HID:, :], low[: 2 * HID - TOP, :]
            up = jnp.concatenate([up0, up1], axis=0)
        else:
            part = parts[s if split is None or s < split else s + 1]
            gate, up = part[:HID, :], part[HID : 2 * HID, :]
        full[...] = SCALE_IN * (dot(wt[0], gate) + dot(wt[1], up))
        for j in range(2):
            rows = slice(j * QUARTER, (j + 1) * QUARTER)
            send[s, rows, :] = full[rows_of(other_if(j, x) * 2 + 1 - c), :].astype(BF16)
            keep[s, rows, :] = full[rows_of(other_if(j, x) * 2 + c), :].astype(BF16)


def token_call(pos, parts, wt, split):
    count = len(parts) - (split is not None)
    shape = sds((count, 2 * QUARTER, GROUP), BF16)
    return call(
        functools.partial(token_kernel, count, split),
        "token",
        10,
        2 * 800 * COLS * GROUP * count,
        9 << 20,
        (shape, shape),
        (pos, *parts, wt),
        in_specs=[SMEM] + [VMEM] * (len(parts) + 1),
        scratch_shapes=[pltpu.VMEM((COLS, GROUP), F32)],
    )


def lay(own, before, after_, far_top, far_low, grads):
    grads[:, :GROUP] = own[...]
    grads[:, GROUP : 2 * GROUP] = after_[...]
    grads[:TOP, 2 * GROUP : 3 * GROUP] = far_top[...]
    grads[TOP:, 2 * GROUP : 3 * GROUP] = far_low[...]
    grads[:, 3 * GROUP :] = before[...]


def weight_kernel(own, before, after_, far_top, far_low, tk, og, out, grads):
    lay(own, before, after_, far_top, far_low, grads)
    out[0] = dot_lanes(grads[:HID, :], tk[...])
    out[1] = dot_lanes(grads[HID : 2 * HID, :], tk[...])
    out[2] = dot_lanes(grads[2 * HID :, :], og[...])


def weight_call(parts, tk, og):
    return call(
        weight_kernel,
        "weight",
        18,
        2 * ROWS * COLS * 1024,
        9 << 20,
        sds((3, HID, COLS), F32),
        (*parts, tk, og),
        scratch_shapes=[pltpu.VMEM((ROWS, 4 * GROUP), BF16)],
    )


def more_kernel(own, before, after_, tk, og, first_sum, out, grads):
    grads[:, :GROUP] = own[...]
    grads[:, GROUP : 2 * GROUP] = after_[...]
    grads[:, 2 * GROUP :] = before[...]
    for i, ref in enumerate((tk, tk, og)):
        rows = slice(i * HID, (i + 1) * HID)
        part = dot_lanes(grads[rows, : 2 * GROUP], ref[:, : 2 * GROUP])
        part += dot_lanes(grads[rows, 2 * GROUP :], ref[:, 3 * GROUP :])
        out[i] = first_sum[i] + part


def more_call(own, before, after_, tk, og, first_sum):
    return call(
        more_kernel,
        "more",
        20,
        2 * ROWS * COLS * 768,
        12 << 20,
        sds((3, HID, COLS), F32),
        (own, before, after_, tk, og, first_sum),
        scratch_shapes=[pltpu.VMEM((ROWS, 3 * GROUP), BF16)],
    )


BLOCK = 40


def step_kernel(far_top, far_low, tk, og, first_sum, master, m1, m2, update, squares, total):
    lanes = slice(2 * GROUP, 3 * GROUP)
    up = jnp.concatenate([far_top[HID:, :], far_low[: 2 * HID - TOP, :]], axis=0)
    for i, (part, ref) in enumerate(((far_top[:HID, :], tk), (up, tk), (far_low[2 * HID - TOP :, :], og))):
        scale = SCALE_OUT if i == 2 else SCALE_IN
        total[...] = dot_lanes(part, ref[:, lanes])

        def block(n, running):
            rows = pl.ds(pl.multiple_of(n * BLOCK, 8), BLOCK)
            gradient = scale * (first_sum[i, rows, :] + total[rows, :])
            new_first = beta_first * m1[i, rows, :] + (1.0 - beta_first) * gradient
            new_second = beta_second * m2[i, rows, :] + (1.0 - beta_second) * gradient * gradient
            first_hat = new_first * (1.0 / (1.0 - beta_first**step_power))
            second_hat = new_second * (1.0 / (1.0 - beta_second**step_power))
            result = first_hat / (jnp.sqrt(second_hat) + epsilon) + weight_decay * master[i, rows, :]
            update[i, rows, :] = result
            return running + fold(result * result)

        squares[i] = lax.fori_loop(0, HID // BLOCK, block, jnp.zeros((8, COLS), F32))


def step_call(far, tk, og, first_sum, master, m1, m2):
    return call(
        step_kernel,
        "step",
        26,
        2 * ROWS * COLS * 256,
        19 << 20,
        (sds((3, HID, COLS), F32), sds((3, 8, COLS), F32)),
        (*far, tk, og, first_sum, master, m1, m2),
        scratch_shapes=[pltpu.VMEM((HID, COLS), F32)],
    )


def squares_kernel(weights, updates, out):
    lane = lax.broadcasted_iota(jnp.int32, (8, 128), 1)
    values = jnp.zeros((8, 128), F32)
    for i in range(3):
        for j, ref in enumerate((weights, updates)):
            values = jnp.where(lane == 2 * i + j, jnp.sum(ref[i]), values)
    for n in range(32):
        out[n] = values


def squares_call(weights, updates, deps):
    return call(squares_kernel, "squares", 2, 1 << 10, 1 << 18, sds((32, 8, 128), F32), (weights, updates), deps)


def total_kernel(parts, out):
    values = jnp.sum(parts[...], axis=0)
    for n in range(8):
        out[n] = values


def total_call(parts, deps):
    return call(total_kernel, "total", 2, 1 << 10, 1 << 18, sds((8, 8, 128), F32), (parts,), deps)


def quarter_kernel(keep, got, out):
    out[...] = (keep[...] + got[...].astype(F32)).astype(BF16)


def quarter_call(keep, got, deps):
    return call(quarter_kernel, "quarter", 4, 1 << 10, 1 << 20, sds(got.shape, BF16), (keep, got), deps)


def z_send(value, k):
    return lax.ppermute(value, "tensor", z_shift(k))


NEAR = (0, 1, -1, 2)
FAR = (-2, 3, -3, 4)


def z_home(value, offsets, k):
    pairs = [
        (dp_index(y, h) * 32 + tp_index(z, x, c), dp_index(y, h) * 32 + tp_index(z + offsets[(y + k) % 4], x, c))
        for y, h in DP
        for z, x, c in TP
    ]
    return lax.ppermute(value, ("dp", "tensor"), pairs)


def local(tokens, out_grad, master, moment_first, moment_second):
    dp = lax.axis_index("dp")
    tensor = lax.axis_index("tensor")
    h = dp % 2
    pos = jnp.stack([dp // 2, h, (tensor // 2) % 2, tensor % 2]).astype(jnp.int32)
    left_half = h == 0

    piece = jnp.concatenate([after(tokens, pos, left_half).T, out_grad.T], axis=0)
    piece = lax.ppermute(piece, ("dp", "tensor"), TURN)
    wgu, wd, wt, weight_squares = cast_call(master)
    piece = after(piece, wgu, wd, wt, weight_squares)
    held = jnp.concatenate([piece, lax.ppermute(piece, "tensor", X_SWAP)], axis=0)

    up1, down1 = z_send(held, 1), z_send(held, -1)
    up2, down2 = z_send(up1, 1), z_send(down1, -1)
    up3, down3 = z_send(up2, 1), z_send(down2, -1)
    near_groups = (held, down1, up1, down2)

    def swap_core(value):
        return lax.ppermute(value, "tensor", C_SWAP)

    def pre(mine):
        other = [swap_core(v) for v in mine]
        return pre_call(pos, mine, other, wgu, wd)

    def scatter_far(far_top, far_low, plus, minus):
        got_top = lax.ppermute(far_top, "dp", y_shift(1))
        got_low = lax.ppermute(far_low, "dp", y_shift(-1))
        plus = plus.at[:TOP].set((plus[:TOP].astype(F32) + got_top.astype(F32)).astype(BF16))
        minus = minus.at[TOP:].set((minus[TOP:].astype(F32) + got_low.astype(F32)).astype(BF16))
        return plus, minus

    def scatter_near(own, plus, minus):
        from_below = lax.ppermute(plus, "dp", y_shift(1))
        from_above = lax.ppermute(minus, "dp", y_shift(-1))
        total = own + from_below.astype(F32) + from_above.astype(F32)
        left, right = total[:, : GROUP // 2], total[:, GROUP // 2 :]
        keep = jnp.where(left_half, left, right)
        send = jnp.where(left_half, right, left).astype(BF16)
        return keep, send

    def swap_h(value):
        return lax.ppermute(value, "dp", H_SWAP)

    def join(mine):
        other = swap_h(mine)
        return jnp.where(
            left_half, jnp.concatenate([mine, other], axis=1), jnp.concatenate([other, mine], axis=1)
        )

    def gather_near(block):
        return lax.ppermute(block, "dp", y_shift(1)), lax.ppermute(block, "dp", y_shift(-1))

    def gather_far(before, after_):
        return (
            lax.ppermute(before[:TOP], "dp", y_shift(1)),
            lax.ppermute(after_[TOP:], "dp", y_shift(-1)),
        )

    def token_part(parts, split=None):
        send, keep = token_call(pos, parts, wt, split)
        part = keep.astype(F32) + swap_core(send).astype(F32)
        got = lax.ppermute(part[:, QUARTER:].astype(BF16), "tensor", X_SWAP)
        return part[:, :QUARTER], got

    def token_sum(part, homes, deps):
        part = quarter_call(*part, deps)
        got = [z_home(part[i], offsets, k) for i, (offsets, k) in enumerate(homes)]
        return sum(v.astype(F32) for v in got)

    tk1, og1, own1, plus1, minus1, far_top1, far_low1 = pre(near_groups)
    up3, down3 = after(up3, far_top1), after(down3, far_top1)
    half = 2 * QUARTER
    across = jnp.concatenate([z_send(up3[:half], 1), z_send(down3[half:], -1)], axis=0)
    plus1, minus1 = scatter_far(far_top1, far_low1, plus1, minus1)
    across = after(across, plus1, minus1)
    tk2, og2, own2, plus2, minus2, far_top2, far_low2 = pre((up2, down3, up3, across))
    keep1, send1 = scatter_near(own1, plus1, minus1)
    plus2, minus2 = scatter_far(far_top2, far_low2, plus2, minus2)
    keep2, send2 = scatter_near(own2, plus2, minus2)
    block1 = join(act_call(keep1, swap_h(send1)))
    send2 = after(send2, block1)
    before1, after1 = gather_near(block1)
    block2 = join(act_call(keep2, swap_h(send2)))
    far1 = gather_far(before1, after1)
    before2, after2 = gather_near(block2)

    early = token_part((block1, after1, before1, *far1), 3)
    first_sum = weight_call((block1, before1, after1, *far1), tk1, og1)
    far2 = gather_far(before2, after2)
    beside = token_part((block2, after2, before2))
    first_sum = more_call(block2, before2, after2, tk2, og2, first_sum)
    last = token_part(far2, 0)
    update, squares = step_call(far2, tk2, og2, first_sum, master, moment_first, moment_second)
    sums = squares_call(weight_squares, squares, ())
    early = token_sum(early, ((NEAR, 0), (NEAR, 1), (NEAR, 3), (NEAR, 2)), (sums,))
    sums = total_call(lax.all_to_all(sums, "tensor", 0, 0), ())
    beside = token_sum(beside, ((FAR, 0), (FAR, 1), (FAR, 3)), (sums,))
    last = token_sum(last, ((FAR, 2),), (sums,))
    token_grad = lax.ppermute((early + beside + last).astype(BF16), ("dp", "tensor"), TURN).T
    sums = jnp.sum(lax.all_to_all(sums, "dp", 0, 0), axis=0)[0, :6].reshape(3, 2)
    trust_ratio = jnp.sqrt(sums[:, 0]) / jnp.sqrt(sums[:, 1])
    return (token_grad, trust_ratio[:, None, None] * update)


def solution(mesh):
    state = P(None, "tensor", "dp")
    rows = P("dp", "tensor")
    return jax.shard_map(
        local,
        mesh=mesh,
        in_specs=(rows, rows, state, state, state),
        out_specs=(rows, state),
        check_vma=False,
    )
```

```python
import functools

import jax
import jax.numpy as jnp
from jax import lax
from jax.experimental import pallas as pl
from jax.experimental.pallas import tpu as pltpu
from jax.sharding import PartitionSpec as P

D = 5120
FF = 12800

beta_first = 0.9
beta_second = 0.95
epsilon = 1e-06
weight_decay = 0.1
step_power = 3.0

SCALE_IN = D ** (-0.5)
SCALE_OUT = FF ** (-0.5)

NY, NH, NZ, NX, NC = 4, 2, 8, 2, 2
HID = 400
COLS = 640
QUARTER = 160
GROUP = 256
TOP = 608
ROWS = 3 * HID
BF16 = jnp.bfloat16
F32 = jnp.float32
MIB = 1 << 20

DP = [(y, h) for y in range(NY) for h in range(NH)]
TP = [(z, x, c) for z in range(NZ) for x in range(NX) for c in range(NC)]


def dp_index(y, h):
    return (y % NY) * NH + h


def tp_index(z, x, c):
    return ((z % NZ) * NX + x) * NC + c


def y_shift(k):
    return [(dp_index(y, h), dp_index(y + k, h)) for y, h in DP]


def z_shift(k):
    return [(tp_index(z, x, c), tp_index(z + k, x, c)) for z, x, c in TP]


H_SWAP = [(dp_index(y, h), dp_index(y, 1 - h)) for y, h in DP]
X_SWAP = [(tp_index(z, x, c), tp_index(z, 1 - x, c)) for z, x, c in TP]
C_SWAP = [(tp_index(z, x, c), tp_index(z, x, 1 - c)) for z, x, c in TP]
TURN = [
    (dp_index(y, h) * 32 + tp_index(z, x, c), z * 32 + tp_index(dp_index(y, h), x, c))
    for y, h in DP
    for z, x, c in TP
]

VMEM = pl.BlockSpec(memory_space=pltpu.VMEM)
SMEM = pl.BlockSpec(memory_space=pltpu.SMEM)


def dot(a, b):
    return lax.dot_general(a, b, (((1,), (0,)), ((), ())), preferred_element_type=F32)


def dot_lanes(a, b):
    return lax.dot_general(a, b, (((1,), (1,)), ((), ())), preferred_element_type=F32)


def other_if(j, x):
    return 1 - x if j else x


def lanes_of(slot):
    return pl.ds(pl.multiple_of(slot * GROUP, GROUP), GROUP)


def rows_of(quarter):
    return pl.ds(pl.multiple_of(quarter * QUARTER, QUARTER), QUARTER)


def after(value, *earlier):
    return lax.optimization_barrier((value,) + earlier)[0]


def call(kernel, name, limit, flops, read, out_shape, args, deps=(), **kw):
    count = len(args)

    def body(*refs):
        kernel(*refs[:count], *refs[count + len(deps) :])

    specs = kw.pop("in_specs", [VMEM] * count) + [pl.BlockSpec(memory_space=pl.ANY)] * len(deps)
    kw.setdefault("out_specs", jax.tree.map(lambda _: VMEM, out_shape))
    return pl.pallas_call(
        body,
        out_shape=out_shape,
        in_specs=specs,
        compiler_params=pltpu.CompilerParams(vmem_limit_bytes=limit * MIB),
        cost_estimate=pl.CostEstimate(flops=flops, bytes_accessed=read, transcendentals=0),
        name=name,
        **kw,
    )(*args, *deps)


def sds(shape, dtype):
    return jax.ShapeDtypeStruct(shape, dtype)


def fold(values):
    return jnp.sum(values.reshape(-1, 8, COLS), axis=0)


def cast_kernel(master, wgu, wd, wt, squares):
    m = pl.program_id(0)
    values = master[0]
    weights = values.astype(BF16)
    squares[0] = fold(values * values)

    @pl.when(m < 2)
    def _():
        wgu[0] = weights
        wt[0] = weights.T

    @pl.when(m == 2)
    def _():
        wd[...] = weights


def cast_call(master):
    clamp = lambda m: (jnp.minimum(m, 1), 0, 0)
    return call(
        cast_kernel,
        "cast",
        14,
        1 << 20,
        6 << 20,
        (sds((2, HID, COLS), BF16), sds((HID, COLS), BF16), sds((2, COLS, HID), BF16), sds((3, 8, COLS), F32)),
        (master,),
        grid=(3,),
        in_specs=[pl.BlockSpec((1, HID, COLS), lambda m: (m, 0, 0))],
        out_specs=(
            pl.BlockSpec((1, HID, COLS), clamp),
            pl.BlockSpec((HID, COLS), lambda m: (0, 0)),
            pl.BlockSpec((1, COLS, HID), clamp),
            pl.BlockSpec((1, 8, COLS), lambda m: (m, 0, 0)),
        ),
    )


def pre_kernel(pos, m0, m1, m2, m3, o0, o1, o2, o3, wgu, wd, tk, og, own, plus, minus, far_top, far_low):
    y, x, c = pos[0], pos[2], pos[3]
    for s, (mine, other) in enumerate(((m0, o0), (m1, o1), (m2, o2), (m3, o3))):
        lanes = lanes_of(lax.rem(s + 4 - y, 4))
        for ref, core in ((mine, c), (other, 1 - c)):
            for j in range(2):
                rows = rows_of(other_if(j, x) * 2 + core)
                base = j * 2 * QUARTER
                tk[rows, lanes] = ref[base : base + QUARTER, :]
                og[rows, lanes] = ref[base + QUARTER : base + 2 * QUARTER, :]
    for k in (2, 1, 3, 0):
        lanes = slice(k * GROUP, (k + 1) * GROUP)
        gate = SCALE_IN * dot(wgu[0], tk[:, lanes])
        up = SCALE_IN * dot(wgu[1], tk[:, lanes])
        hid = SCALE_OUT * dot(wd[...], og[:, lanes])
        if k == 2:
            far_top[:HID, :] = gate.astype(BF16)
            far_top[HID:, :] = up[: TOP - HID].astype(BF16)
            far_low[: 2 * HID - TOP, :] = up[TOP - HID :].astype(BF16)
            far_low[2 * HID - TOP :, :] = hid.astype(BF16)
        else:
            out = (own, plus, None, minus)[k]
            out[:HID, :] = gate.astype(out.dtype)
            out[HID : 2 * HID, :] = up.astype(out.dtype)
            out[2 * HID :, :] = hid.astype(out.dtype)


def pre_call(pos, mine, other, wgu, wd):
    return call(
        pre_kernel,
        "pre",
        14,
        2 * ROWS * COLS * 1024,
        9 << 20,
        (
            sds((COLS, 4 * GROUP), BF16),
            sds((COLS, 4 * GROUP), BF16),
            sds((ROWS, GROUP), F32),
            sds((ROWS, GROUP), BF16),
            sds((ROWS, GROUP), BF16),
            sds((TOP, GROUP), BF16),
            sds((ROWS - TOP, GROUP), BF16),
        ),
        (pos, *mine, *other, wgu, wd),
        in_specs=[SMEM] + [VMEM] * 10,
    )


def act_kernel(keep, recv, out):
    gate = keep[:HID, :] + recv[:HID, :].astype(F32)
    up = keep[HID : 2 * HID, :] + recv[HID : 2 * HID, :].astype(F32)
    hid = keep[2 * HID :, :] + recv[2 * HID :, :].astype(F32)
    sig = jax.nn.sigmoid(gate)
    swish = gate * sig
    out[:HID, :] = (hid * up * sig * (1.0 + gate * (1.0 - sig))).astype(BF16)
    out[HID : 2 * HID, :] = (hid * swish).astype(BF16)
    out[2 * HID :, :] = (swish * up).astype(BF16)


def act_call(keep, recv):
    return call(act_kernel, "act", 6, HID * 128 * 40, 2 << 20, sds((ROWS, GROUP // 2), BF16), (keep, recv))


def token_kernel(count, split, pos, *refs):
    parts, (wt, send, keep, full) = refs[:-4], refs[-4:]
    x, c = pos[2], pos[3]
    for s in range(count):
        if s == split:
            top, low = parts[s], parts[s + 1]
            gate, up0, up1 = top[:HID, :], top[HID:, :], low[: 2 * HID - TOP, :]
            up = jnp.concatenate([up0, up1], axis=0)
        else:
            part = parts[s if split is None or s < split else s + 1]
            gate, up = part[:HID, :], part[HID : 2 * HID, :]
        full[...] = SCALE_IN * (dot(wt[0], gate) + dot(wt[1], up))
        for j in range(2):
            rows = slice(j * QUARTER, (j + 1) * QUARTER)
            send[s, rows, :] = full[rows_of(other_if(j, x) * 2 + 1 - c), :].astype(BF16)
            keep[s, rows, :] = full[rows_of(other_if(j, x) * 2 + c), :].astype(BF16)


def token_call(pos, parts, wt, split):
    count = len(parts) - (split is not None)
    shape = sds((count, 2 * QUARTER, GROUP), BF16)
    return call(
        functools.partial(token_kernel, count, split),
        "token",
        10,
        2 * 800 * COLS * GROUP * count,
        9 << 20,
        (shape, shape),
        (pos, *parts, wt),
        in_specs=[SMEM] + [VMEM] * (len(parts) + 1),
        scratch_shapes=[pltpu.VMEM((COLS, GROUP), F32)],
    )


def lay(own, before, after_, far_top, far_low, grads):
    grads[:, :GROUP] = own[...]
    grads[:, GROUP : 2 * GROUP] = after_[...]
    grads[:TOP, 2 * GROUP : 3 * GROUP] = far_top[...]
    grads[TOP:, 2 * GROUP : 3 * GROUP] = far_low[...]
    grads[:, 3 * GROUP :] = before[...]


def weight_kernel(own, before, after_, far_top, far_low, tk, og, out, grads):
    lay(own, before, after_, far_top, far_low, grads)
    out[0] = dot_lanes(grads[:HID, :], tk[...])
    out[1] = dot_lanes(grads[HID : 2 * HID, :], tk[...])
    out[2] = dot_lanes(grads[2 * HID :, :], og[...])


def weight_call(parts, tk, og):
    return call(
        weight_kernel,
        "weight",
        18,
        2 * ROWS * COLS * 1024,
        9 << 20,
        sds((3, HID, COLS), F32),
        (*parts, tk, og),
        scratch_shapes=[pltpu.VMEM((ROWS, 4 * GROUP), BF16)],
    )


def more_kernel(own, before, after_, tk, og, first_sum, out, grads):
    grads[:, :GROUP] = own[...]
    grads[:, GROUP : 2 * GROUP] = after_[...]
    grads[:, 2 * GROUP :] = before[...]
    for i, ref in enumerate((tk, tk, og)):
        rows = slice(i * HID, (i + 1) * HID)
        part = dot_lanes(grads[rows, : 2 * GROUP], ref[:, : 2 * GROUP])
        part += dot_lanes(grads[rows, 2 * GROUP :], ref[:, 3 * GROUP :])
        out[i] = first_sum[i] + part


def more_call(own, before, after_, tk, og, first_sum):
    return call(
        more_kernel,
        "more",
        20,
        2 * ROWS * COLS * 768,
        12 << 20,
        sds((3, HID, COLS), F32),
        (own, before, after_, tk, og, first_sum),
        scratch_shapes=[pltpu.VMEM((ROWS, 3 * GROUP), BF16)],
    )


BLOCK = 40


def step_kernel(far_top, far_low, tk, og, first_sum, master, m1, m2, update, squares, total):
    lanes = slice(2 * GROUP, 3 * GROUP)
    up = jnp.concatenate([far_top[HID:, :], far_low[: 2 * HID - TOP, :]], axis=0)
    for i, (part, ref) in enumerate(((far_top[:HID, :], tk), (up, tk), (far_low[2 * HID - TOP :, :], og))):
        scale = SCALE_OUT if i == 2 else SCALE_IN
        total[...] = dot_lanes(part, ref[:, lanes])

        def block(n, running):
            rows = pl.ds(pl.multiple_of(n * BLOCK, 8), BLOCK)
            gradient = scale * (first_sum[i, rows, :] + total[rows, :])
            new_first = beta_first * m1[i, rows, :] + (1.0 - beta_first) * gradient
            new_second = beta_second * m2[i, rows, :] + (1.0 - beta_second) * gradient * gradient
            first_hat = new_first * (1.0 / (1.0 - beta_first**step_power))
            second_hat = new_second * (1.0 / (1.0 - beta_second**step_power))
            result = first_hat / (jnp.sqrt(second_hat) + epsilon) + weight_decay * master[i, rows, :]
            update[i, rows, :] = result
            return running + fold(result * result)

        squares[i] = lax.fori_loop(0, HID // BLOCK, block, jnp.zeros((8, COLS), F32))


def step_call(far, tk, og, first_sum, master, m1, m2):
    return call(
        step_kernel,
        "step",
        26,
        2 * ROWS * COLS * 256,
        19 << 20,
        (sds((3, HID, COLS), F32), sds((3, 8, COLS), F32)),
        (*far, tk, og, first_sum, master, m1, m2),
        scratch_shapes=[pltpu.VMEM((HID, COLS), F32)],
    )


def squares_kernel(weights, updates, out):
    lane = lax.broadcasted_iota(jnp.int32, (8, 128), 1)
    values = jnp.zeros((8, 128), F32)
    for i in range(3):
        for j, ref in enumerate((weights, updates)):
            values = jnp.where(lane == 2 * i + j, jnp.sum(ref[i]), values)
    for n in range(32):
        out[n] = values


def squares_call(weights, updates, deps):
    return call(squares_kernel, "squares", 2, 1 << 10, 1 << 18, sds((32, 8, 128), F32), (weights, updates), deps)


def total_kernel(parts, out):
    values = jnp.sum(parts[...], axis=0)
    for n in range(8):
        out[n] = values


def total_call(parts, deps):
    return call(total_kernel, "total", 2, 1 << 10, 1 << 18, sds((8, 8, 128), F32), (parts,), deps)


def quarter_kernel(keep, got, out):
    out[...] = (keep[...] + got[...].astype(F32)).astype(BF16)


def quarter_call(keep, got, deps):
    return call(quarter_kernel, "quarter", 4, 1 << 10, 1 << 20, sds(got.shape, BF16), (keep, got), deps)


def slots_kernel(pos, keep, got, out):
    for i, k in enumerate((0, 1, 3, 2)):
        out[lax.rem(pos[0] + k, 4)] = (keep[i] + got[i].astype(F32)).astype(BF16)


def slots_call(pos, keep, got, deps):
    shape = sds(got.shape, BF16)
    specs = [SMEM, VMEM, VMEM]
    return call(slots_kernel, "slots", 4, 1 << 10, 1 << 20, shape, (pos, keep, got), deps, in_specs=specs)


def z_send(value, k):
    return lax.ppermute(value, "tensor", z_shift(k))


NEAR = (0, 1, -1, 2)
FAR = (-2, 3, -3, 4)


def z_home(value, offsets, k):
    pairs = [
        (dp_index(y, h) * 32 + tp_index(z, x, c), dp_index(y, h) * 32 + tp_index(z + offsets[(y + k) % 4], x, c))
        for y, h in DP
        for z, x, c in TP
    ]
    return lax.ppermute(value, ("dp", "tensor"), pairs)


def local(tokens, out_grad, master, moment_first, moment_second):
    dp = lax.axis_index("dp")
    tensor = lax.axis_index("tensor")
    h = dp % 2
    pos = jnp.stack([dp // 2, h, (tensor // 2) % 2, tensor % 2]).astype(jnp.int32)
    left_half = h == 0

    piece = jnp.concatenate([after(tokens, pos, left_half).T, out_grad.T], axis=0)
    piece = lax.ppermute(piece, ("dp", "tensor"), TURN)
    wgu, wd, wt, weight_squares = cast_call(master)
    piece = after(piece, wgu, wd, wt, weight_squares)
    held = jnp.concatenate([piece, lax.ppermute(piece, "tensor", X_SWAP)], axis=0)

    up1, down1 = z_send(held, 1), z_send(held, -1)
    up2, down2 = z_send(up1, 1), z_send(down1, -1)
    up3, down3 = z_send(up2, 1), z_send(down2, -1)
    near_groups = (held, down1, up1, down2)

    def swap_core(value):
        return lax.ppermute(value, "tensor", C_SWAP)

    def pre(mine):
        other = [swap_core(v) for v in mine]
        return pre_call(pos, mine, other, wgu, wd)

    def scatter_far(far_top, far_low, plus, minus):
        got_top = lax.ppermute(far_top, "dp", y_shift(1))
        got_low = lax.ppermute(far_low, "dp", y_shift(-1))
        plus = plus.at[:TOP].set((plus[:TOP].astype(F32) + got_top.astype(F32)).astype(BF16))
        minus = minus.at[TOP:].set((minus[TOP:].astype(F32) + got_low.astype(F32)).astype(BF16))
        return plus, minus

    def scatter_near(own, plus, minus):
        from_below = lax.ppermute(plus, "dp", y_shift(1))
        from_above = lax.ppermute(minus, "dp", y_shift(-1))
        total = own + from_below.astype(F32) + from_above.astype(F32)
        left, right = total[:, : GROUP // 2], total[:, GROUP // 2 :]
        keep = jnp.where(left_half, left, right)
        send = jnp.where(left_half, right, left).astype(BF16)
        return keep, send

    def swap_h(value):
        return lax.ppermute(value, "dp", H_SWAP)

    def join(mine):
        other = swap_h(mine)
        return jnp.where(
            left_half, jnp.concatenate([mine, other], axis=1), jnp.concatenate([other, mine], axis=1)
        )

    def gather_near(block):
        return lax.ppermute(block, "dp", y_shift(1)), lax.ppermute(block, "dp", y_shift(-1))

    def gather_far(before, after_):
        return (
            lax.ppermute(before[:TOP], "dp", y_shift(1)),
            lax.ppermute(after_[TOP:], "dp", y_shift(-1)),
        )

    def token_part(parts, split=None):
        send, keep = token_call(pos, parts, wt, split)
        part = keep.astype(F32) + swap_core(send).astype(F32)
        got = lax.ppermute(part[:, QUARTER:].astype(BF16), "tensor", X_SWAP)
        return part[:, :QUARTER], got

    def token_sum(part, homes, deps):
        part = quarter_call(*part, deps)
        got = [z_home(part[i], offsets, k) for i, (offsets, k) in enumerate(homes)]
        return sum(v.astype(F32) for v in got)

    tk1, og1, own1, plus1, minus1, far_top1, far_low1 = pre(near_groups)
    up3, down3 = after(up3, far_top1), after(down3, far_top1)
    half = 2 * QUARTER
    across = jnp.concatenate([z_send(up3[:half], 1), z_send(down3[half:], -1)], axis=0)
    plus1, minus1 = scatter_far(far_top1, far_low1, plus1, minus1)
    across = after(across, plus1, minus1)
    tk2, og2, own2, plus2, minus2, far_top2, far_low2 = pre((up2, down3, up3, across))
    keep1, send1 = scatter_near(own1, plus1, minus1)
    plus2, minus2 = scatter_far(far_top2, far_low2, plus2, minus2)
    keep2, send2 = scatter_near(own2, plus2, minus2)
    block1 = join(act_call(keep1, swap_h(send1)))
    send2 = after(send2, block1)
    before1, after1 = gather_near(block1)
    block2 = join(act_call(keep2, swap_h(send2)))
    far1 = gather_far(before1, after1)
    before2, after2 = gather_near(block2)

    early = token_part((block1, after1, before1, *far1), 3)
    first_sum = weight_call((block1, before1, after1, *far1), tk1, og1)
    far2 = gather_far(before2, after2)
    beside = token_part((block2, after2, before2))
    first_sum = more_call(block2, before2, after2, tk2, og2, first_sum)
    last = token_part(far2, 0)
    update, squares = step_call(far2, tk2, og2, first_sum, master, moment_first, moment_second)
    sums = squares_call(weight_squares, squares, ())
    early = slots_call(pos, *early, (sums,))
    early = sum((z_send(early[i], k) if k else early[i]).astype(F32) for i, k in enumerate(NEAR))
    sums = total_call(lax.all_to_all(sums, "tensor", 0, 0), ())
    beside = token_sum(beside, ((FAR, 0), (FAR, 1), (FAR, 3)), (sums,))
    last = token_sum(last, ((FAR, 2),), (sums,))
    token_grad = lax.ppermute((early + beside + last).astype(BF16), ("dp", "tensor"), TURN).T
    sums = jnp.sum(lax.all_to_all(sums, "dp", 0, 0), axis=0)[0, :6].reshape(3, 2)
    trust_ratio = jnp.sqrt(sums[:, 0]) / jnp.sqrt(sums[:, 1])
    return (token_grad, trust_ratio[:, None, None] * update)


def solution(mesh):
    state = P(None, "tensor", "dp")
    rows = P("dp", "tensor")
    return jax.shard_map(
        local,
        mesh=mesh,
        in_specs=(rows, rows, state, state, state),
        out_specs=(rows, state),
        check_vma=False,
    )
```
